1024 devices in a mesh: gx: 64 (over z, x), gy: 16 (over y, core).
Axes of the slice: x: 8, y: 8, z: 8, core: 2. Of those that a mesh axis runs over, the one named last changes fastest.
Arguments:
- background: float32 [2048, 16, 2048], P('gx', None, 'gy'), may hold values from -6 to 6
- nearbody: float32 [2, 1024, 16, 2048], P(None, 'gx', None, 'gy'), may hold values from -6 to 6
- donor_rows: int32 [64, 16, 64, 2], P('gx', 'gy'), may hold values from -1 to 479, as said below
- donor_fractions: float32 [3, 64, 16, 64, 2], P(None, 'gx', 'gy'), may hold values from 0 to 1
- fringe_slots: int32 [64, 16, 64, 2], P('gx', 'gy'), may hold values from -1 to 511, as said below
- return_rows: int32 [64, 16, 64, 2], P('gx', 'gy'), may hold values from -1 to 415, as said below
- return_fractions: float32 [3, 64, 16, 64, 2], P(None, 'gx', 'gy'), may hold values from 0 to 1
- hole_slots: int32 [64, 16, 64, 2], P('gx', 'gy'), may hold values from -1 to 511, as said below
Outputs:
- back_field: float32 [2048, 16, 2048], P('gx', None, 'gy')
- body_field: float32 [2, 1024, 16, 2048], P(None, 'gx', None, 'gy')
The draws below stay inside these ranges and needn't reach their ends.
Inputs may be any that keep to these rules, and one draw needn't show every extreme that they name: Entry [q, j, p, s] is -1 where the slot is empty, else a row index. For each owner p and column j the sources with nonempty slots each fill exactly all 2 slots, and there are 32 of them; donor_rows[q, j, p, s] >= 0 exactly where fringe_slots[p, j, q, s] >= 0. `fringe_slots`: entry [p, j, q, s] is -1 or a fringe row (g * 16 + i) * 16 + k with k one of the two outermost layers 14, 15; every one of these 64 rows of a device appears exactly once. Entry [p, j, q, s] is -1 where the slot is empty, else a row index. For each background owner q and column j the sources with nonempty slots each fill exactly all 2 slots, and there are 32 of them; return_rows[p, j, q, s] >= 0 exactly where hole_slots[q, j, p, s] >= 0. `hole_slots`: entry [q, j, p, s] is -1 or a background row x 16 + z of the device; each device receives exactly 64 distinct rows.
All inputs are finite; a program needn't handle non-finite values.
Results may differ from the reference program's by a relative error of at most 0.0003.
Values sent between devices are 32-bit elements; how exact they have to be, the bound alone decides.
A program may use at most 32 MiB of HBM per device.

```python
import jax
import jax.numpy as jnp
from jax import lax

BX = 32
BZ = 16
BY = 128
HX = 16
HZ = 16
STEPS = 2
C = 2
NXB = 2048
NYB = 2048
NHX = 1024
N_GX = 64
N_GY = 16


def routing(key, salt, targets, row_range):
    key = jax.random.fold_in(key, salt)
    key_centre, key_jitter, key_order, key_rows = jax.random.split(key, 4)
    row_total = 4 * HX
    pair_count = row_total // C
    centre = jax.random.randint(key_centre, (N_GY,), 0, N_GX)
    source = jnp.arange(N_GX)
    distance = jnp.abs(source[None, :] - centre[:, None])
    distance = jnp.minimum(distance, N_GX - distance)
    jitter = jax.random.randint(key_jitter, (N_GX, N_GY, N_GX), 0, 2 * N_GX)
    scores = (jitter + 2 * (N_GX // 2 - distance)[None]) * N_GX + source[None, None, :]
    chosen = lax.top_k(scores, pair_count)[1]
    key_list = jax.random.split(key_order, N_GX * N_GY)
    orders = jax.vmap(lambda member: jax.random.permutation(member, row_total))(key_list).reshape(N_GX, N_GY, row_total)
    position = jnp.arange(row_total)
    sender = chosen[:, :, position // C]
    slot_index = position % C
    target = jnp.take_along_axis(targets, orders, axis=2)
    receive = jnp.full((N_GX, N_GY, N_GX, C), -1, jnp.int32)
    receive = receive.at[jnp.arange(N_GX)[:, None, None], jnp.arange(N_GY)[None, :, None], sender, slot_index[None, None, :]].set(target.astype(jnp.int32))
    picked = jax.random.randint(key_rows, (N_GX, N_GY, N_GX, C), 0, row_range)
    outgoing = jnp.where(jnp.transpose(receive, (2, 1, 0, 3)) >= 0, picked, -1)
    return (receive, outgoing.astype(jnp.int32))


def outer_rows():
    position = jnp.arange(4 * HX)
    grid_id = position // (2 * HX)
    cycle_id = position // 2 % HX
    depth_id = HZ - 1 - position % 2
    flat_rows = (grid_id * HX + cycle_id) * HZ + depth_id
    return jnp.broadcast_to(flat_rows, (N_GX, N_GY, 4 * HX))


def hole_rows(key):
    key = jax.random.fold_in(key, 31)
    key_list = jax.random.split(key, N_GX * N_GY)
    shuffled = jax.vmap(lambda member: jax.random.permutation(member, BX * BZ)[:4 * HX])(key_list)
    return shuffled.reshape(N_GX, N_GY, 4 * HX)


def draw_donor_rows(key, part):
    return routing(key, 11, outer_rows(), BX * (BZ - 1))[1]


def draw_fringe_slots(key, part):
    return routing(key, 11, outer_rows(), BX * (BZ - 1))[0]


def draw_return_rows(key, part):
    return routing(key, 12, hole_rows(key), 2 * HX * (HZ - 3))[1]


def draw_hole_slots(key, part):
    return routing(key, 12, hole_rows(key), 2 * HX * (HZ - 3))[0]


def levels(rng, extent, cuts, smallest, high):
    level = 1.0
    for dim, blocks in cuts:
        draws = jax.random.uniform(jax.random.fold_in(jax.random.fold_in(rng, 6), dim), (blocks,), jnp.float32, smallest / len(cuts), high / len(cuts))
        level = level * jnp.repeat(jnp.exp(draws), extent[dim] // blocks).reshape((-1,) + (1,) * (len(extent) - 1 - dim))
    return level


def noise(stream_key, extent, scale, limit, cuts=(), kind=jnp.bfloat16):
    factor_of = levels(stream_key, extent, cuts, -0.22, 0.18) if cuts else 1.0
    result = jax.random.normal(stream_key, extent, jnp.float32) * scale * factor_of
    return jnp.minimum(jnp.maximum(result, -limit), limit).astype(kind)


def setup_inputs(seed: int = 0) -> dict:
    streams_of = jax.random.split(jax.random.key(seed), 9)
    background = noise(streams_of[0], (NXB, BZ, NYB), 1.0, 6.0, ((0, 64), (2, 16)), jnp.float32)
    nearbody = noise(streams_of[1], (2, NHX, HZ, NYB), 1.0, 6.0, ((1, 64), (3, 16)), jnp.float32)
    donor_rows = draw_donor_rows(jax.random.fold_in(streams_of[8], 71), 0)
    donor_fractions = jnp.clip(1.0 * jax.random.uniform(streams_of[3], (3, N_GX, N_GY, N_GX, C), jnp.float32) ** levels(streams_of[3], (3, N_GX, N_GY, N_GX, C), ((1, 64), (2, 16)), -0.2, 0.2), 0.0, 1.0)
    fringe_slots = draw_fringe_slots(jax.random.fold_in(streams_of[8], 71), 0)
    return_rows = draw_return_rows(jax.random.fold_in(streams_of[8], 71), 0)
    return_fractions = jnp.clip(1.0 * jax.random.uniform(streams_of[6], (3, N_GX, N_GY, N_GX, C), jnp.float32) ** levels(streams_of[6], (3, N_GX, N_GY, N_GX, C), ((1, 64), (2, 16)), -0.2, 0.2), 0.0, 1.0)
    hole_slots = draw_hole_slots(jax.random.fold_in(streams_of[8], 71), 0)
    return dict(background=background, nearbody=nearbody, donor_rows=donor_rows, donor_fractions=donor_fractions, fringe_slots=fringe_slots, return_rows=return_rows, return_fractions=return_fractions, hole_slots=hole_slots)


back_courant = (0.3, 0.25, 0.15)
back_diffuse = 0.04
body_courant = (0.2, 0.3, 0.2)
body_diffuse = 0.045


def advance(padded, courant, diffuse):
    centre = padded[..., 1:-1, 1:-1, 1:-1]
    back_x = padded[..., :-2, 1:-1, 1:-1]
    ahead_x = padded[..., 2:, 1:-1, 1:-1]
    back_z = padded[..., 1:-1, :-2, 1:-1]
    ahead_z = padded[..., 1:-1, 2:, 1:-1]
    back_y = padded[..., 1:-1, 1:-1, :-2]
    ahead_y = padded[..., 1:-1, 1:-1, 2:]
    upwind = courant[0] * (centre - back_x) + courant[1] * (centre - back_y) + courant[2] * (centre - back_z)
    spread = back_x + ahead_x + back_y + ahead_y + back_z + ahead_z - 6.0 * centre
    return centre - upwind + diffuse * spread


def trilinear(field, first_row, second_row, fraction_a, fraction_b, fraction_y, row_length):
    blended = None
    for shift_a in (0, 1):
        weight_a = fraction_a if shift_a else 1.0 - fraction_a
        for shift_b in (0, 1):
            weight_b = fraction_b if shift_b else 1.0 - fraction_b
            picked = field[first_row + shift_a, second_row + shift_b]
            below_y = picked[..., 1:row_length + 1]
            above_y = picked[..., 2:row_length + 2]
            portion = (weight_a * weight_b)[..., None] * ((1.0 - fraction_y)[..., None] * below_y + fraction_y[..., None] * above_y)
            blended = portion if blended is None else blended + portion
    return blended


def reference(background, nearbody, donor_rows, donor_fractions, fringe_slots, return_rows, return_fractions, hole_slots):
    back_field = background
    body_field = nearbody
    columns = jnp.arange(N_GY, dtype=jnp.int32)
    owner = jnp.arange(N_GX, dtype=jnp.int32)[:, None, None]
    layers_used = HZ - 3
    for repeat in range(STEPS):
        moved_back = advance(jnp.pad(back_field, ((1, 1), (1, 1), (1, 1))), back_courant, back_diffuse)
        wrapped = jnp.pad(body_field, ((0, 0), (1, 1), (0, 0), (1, 1)), mode="wrap")
        moved_body = advance(jnp.pad(wrapped, ((0, 0), (0, 0), (1, 1), (0, 0))), body_courant, body_diffuse)
        edged = jnp.pad(back_field, ((1, 1), (0, 0), (1, 1)))
        flat_body = wrapped.reshape(2 * (NHX + 2), HZ, NYB + 2)

        def column_update(column):
            start = column * BY
            back_strip = lax.dynamic_slice_in_dim(edged, start, BY + 2, 2)
            body_strip = lax.dynamic_slice_in_dim(flat_body, start, BY + 2, 2)
            donor_index = jnp.maximum(donor_rows[:, column], 0)
            donor_share = donor_fractions[:, :, column]
            donor_values = trilinear(back_strip, owner * BX + donor_index // (BZ - 1) + 1, donor_index % (BZ - 1),
                                     donor_share[0], donor_share[1], donor_share[2], BY)
            return_index = jnp.maximum(return_rows[:, column], 0)
            return_share = return_fractions[:, :, column]
            return_first = (return_index // (HX * layers_used)) * (NHX + 2) + owner * HX + (return_index // layers_used) % HX + 1
            return_values = trilinear(body_strip, return_first, return_index % layers_used,
                                      return_share[0], return_share[1], return_share[2], BY)
            body_column = lax.dynamic_slice_in_dim(moved_body, start, BY, 3).reshape(2 * NHX * HZ, BY)
            fringe_now = fringe_slots[:, column]
            fringe_spot = (fringe_now // (HX * HZ)) * (NHX * HZ) + owner * (HX * HZ) + fringe_now % (HX * HZ)
            fringe_spot = jnp.where(fringe_now >= 0, fringe_spot, 2 * NHX * HZ)
            body_column = body_column.at[fringe_spot.reshape(-1)].set(
                jnp.transpose(donor_values, (1, 0, 2, 3)).reshape(-1, BY), mode="drop")
            back_column = lax.dynamic_slice_in_dim(moved_back, start, BY, 2).reshape(NXB * BZ, BY)
            hole_now = hole_slots[:, column]
            hole_spot = jnp.where(hole_now >= 0, owner * (BX * BZ) + hole_now, NXB * BZ)
            back_column = back_column.at[hole_spot.reshape(-1)].set(
                jnp.transpose(return_values, (1, 0, 2, 3)).reshape(-1, BY), mode="drop")
            return back_column.reshape(NXB, BZ, BY), body_column.reshape(2, NHX, HZ, BY)

        back_columns, body_columns = lax.map(column_update, columns)
        back_field = jnp.transpose(back_columns, (1, 2, 0, 3)).reshape(NXB, BZ, NYB)
        body_field = jnp.transpose(body_columns, (1, 2, 3, 0, 4)).reshape(2, NHX, HZ, NYB)
    return back_field, body_field
```

```python
import functools

import jax
import jax.numpy as jnp
from jax import lax
from jax.experimental import pallas as pl
from jax.experimental.pallas import tpu as pltpu
from jax.sharding import PartitionSpec as P

STEPS = 2
MESH = pl.DeviceIdType.MESH

BACK = (0.3, 0.25, 0.15, 0.04)
BODY = (0.2, 0.3, 0.2, 0.045)

GROUPS = ((1, 32, 0), (35, 16, 32), (53, 16, 48))
PLANES = 70
Z = 16
LANES = 128
F32 = jnp.float32
BF16 = jnp.bfloat16


def iota(shape, dim):
    return lax.broadcasted_iota(jnp.int32, shape, dim)


def split(value):
    high = value.astype(BF16)
    return high, (value - high.astype(F32)).astype(BF16)


def dot(a, b):
    return jnp.dot(a, b, preferred_element_type=F32)


def exact_dot(a, b, dims=((1,), (0,))):
    return lax.dot_general(
        a, b, (dims, ((), ())), precision=lax.Precision.HIGHEST, preferred_element_type=F32
    )


def kernel(
    nx,
    ny,
    back_ref,
    body_ref,
    donor_rows,
    donor_fractions,
    fringe_slots,
    return_rows,
    return_fractions,
    hole_slots,
    back_out,
    body_out,
    field,
    moved,
    table,
    w_high,
    w_low,
    w_halo,
    w_x,
    w_z,
    share_y,
    place,
    keep,
    edge,
    edge_above,
    edge_below,
    edge_corner,
    sent,
    got,
    in_sem,
    halo_send,
    halo_recv,
    swap_send,
    swap_recv,
    out_sem,
):
    q = lax.axis_index("gx")
    j = lax.axis_index("gy")
    q_up, q_down = lax.rem(q + 1, nx), lax.rem(q + nx - 1, nx)
    j_up, j_down = lax.rem(j + 1, ny), lax.rem(j + ny - 1, ny)

    loads = [
        pltpu.make_async_copy(back_ref, field.at[0, pl.ds(1, 32)], in_sem.at[0]),
        pltpu.make_async_copy(body_ref.at[0], field.at[0, pl.ds(35, 16)], in_sem.at[1]),
        pltpu.make_async_copy(body_ref.at[1], field.at[0, pl.ds(53, 16)], in_sem.at[2]),
    ]
    for load in loads:
        load.start()

    barrier = pltpu.get_barrier_semaphore()

    def greet(step, carry):
        pl.semaphore_signal(
            barrier, inc=1, device_id={"gx": lax.rem(q + step, nx)}, device_id_type=MESH
        )
        return carry

    lax.fori_loop(1, nx, greet, 0)
    for there in ((q, j_up), (q, j_down), (q_down, j_down), (q_up, j_up)):
        pl.semaphore_signal(
            barrier, inc=1, device_id={"gx": there[0], "gy": there[1]}, device_id_type=MESH
        )

    def halo_copies(now):
        f = field.at[now]
        pairs = []
        for n, (first, count, _) in enumerate(GROUPS):
            pairs.append((f.at[first + count - 1], f.at[first - 1], q_up, j))
            pairs.append((f.at[first], f.at[first + count], q_down, j))
        pairs.append((edge.at[now], edge_below.at[now], q, j_up))
        pairs.append((edge.at[now], edge_above.at[now], q, j_down))
        pairs.append((edge.at[now], edge_corner.at[now], q_down, j_down))
        return [
            pltpu.make_async_remote_copy(
                src_ref=src,
                dst_ref=dst,
                send_sem=halo_send.at[now, n],
                recv_sem=halo_recv.at[now, n],
                device_id={"gx": to_q, "gy": to_j},
                device_id_type=MESH,
            )
            for n, (src, dst, to_q, to_j) in enumerate(pairs)
        ]

    lane = iota((Z, LANES), 1)

    def pack_edges(now):
        packed = jnp.zeros((Z, LANES), F32)
        for first, count, plane in GROUPS:
            for k in range(count):
                spot = 2 * (plane + k)
                rolled = pltpu.roll(field[now, first + k], spot, 1)
                hit = (lane == spot) | (lane == (spot - 1) % LANES)
                packed = jnp.where(hit, rolled, packed)
        edge[now] = packed

    for load in loads:
        load.wait()
    pack_edges(0)
    pl.semaphore_wait(barrier, nx - 1 + 4)
    for copy in halo_copies(0):
        copy.start()

    table[...] = jnp.zeros_like(table)
    half = ((donor_rows, return_rows), (fringe_slots, hole_slots))
    for n, (first, second) in enumerate(half):
        table[4 * n : 4 * n + 2, 0:64] = first[...].astype(F32)
        table[4 * n + 2 : 4 * n + 4, 0:64] = second[...].astype(F32)
    for n in range(3):
        table[8 + 4 * n : 10 + 4 * n, 0:64] = donor_fractions[n]
        table[10 + 4 * n : 12 + 4 * n, 0:64] = return_fractions[n]
    rows = 4 * 64
    spread = (iota((LANES, rows), 1) // 4 == iota((LANES, rows), 0)).astype(F32)
    wide = exact_dot(table[...], spread)
    kind = iota((1, rows), 1) % 4

    def pick(n):
        x = wide[4 * n : 4 * n + 4]
        return jnp.where(
            kind == 0, x[0:1], jnp.where(kind == 1, x[1:2], jnp.where(kind == 2, x[2:3], x[3:4]))
        )

    row = jnp.maximum(pick(0), 0.0)
    slot = pick(1)
    donor = kind < 2
    used = jnp.where(donor, float(Z - 1), float(Z - 3))
    plane = jnp.floor((row + 0.5) / used)
    layer = row - plane * used
    plane = jnp.where(donor, plane, plane + 32.0)
    target = jnp.where(slot < 0.0, -1.0, jnp.where(donor, slot + 512.0, slot))
    columns = jnp.concatenate(
        [plane, layer, pick(2), pick(3), pick(4), jnp.zeros((3, rows), F32)], axis=0
    ).T
    plane_c = columns[:, 0:1].astype(jnp.int32)
    layer_c = columns[:, 1:2].astype(jnp.int32)
    f1, f2, f3 = columns[:, 2:3], columns[:, 3:4], columns[:, 4:5]
    share_y[...] = jnp.broadcast_to(f3, (rows, LANES))
    last = (plane_c == 31) | (plane_c == 47) | (plane_c == 63)
    halo_index = jnp.where(plane_c == 31, 0, jnp.where(plane_c == 47, 1, 2))
    w00, w01 = (1.0 - f1) * (1.0 - f2), (1.0 - f1) * f2
    w10, w11 = f1 * (1.0 - f2), f1 * f2
    base = plane_c * Z + layer_c
    far = jnp.where(last, -1000, base + Z)

    def weigh(n, carry):
        k = iota((rows, LANES), 1) + n * LANES
        w = (
            jnp.where(k == base, w00, 0.0)
            + jnp.where(k == base + 1, w01, 0.0)
            + jnp.where(k == far, w10, 0.0)
            + jnp.where(k == far + 1, w11, 0.0)
        )
        high, low = split(w)
        w_high[n] = high
        w_low[n] = low
        return carry

    lax.fori_loop(0, 8, weigh, 0)
    k = iota((rows, LANES), 1)
    near = jnp.where(last, halo_index * Z + layer_c, -1000)
    w_halo[...] = jnp.where(k == near, w10, 0.0) + jnp.where(k == near + 1, w11, 0.0)
    beyond = jnp.where(last, 1 + 2 * halo_index, 2 * plane_c + 2)
    w_x[...] = jnp.where(k == 2 * plane_c, 1.0 - f1, 0.0) + jnp.where(k == beyond, f1, 0.0)
    w_z[...] = jnp.where(k == layer_c, 1.0 - f2, 0.0) + jnp.where(k == layer_c + 1, f2, 0.0)

    target_i = target.astype(jnp.int32)
    ones = jnp.ones((rows, LANES), BF16)

    def lay_back(n, carry):
        r = iota((LANES, rows), 0) + n * LANES
        hit = jnp.where(r == target_i, 1.0, 0.0).astype(BF16)
        place[n] = hit
        keep[n] = 1.0 - dot(hit, ones)
        return carry

    lax.fori_loop(0, 4, lay_back, 0)

    def lay_body(n, carry):
        r = iota((LANES, rows), 0)
        r = 512 + (r // 8 + n * 16) * Z + 8 + r % 8
        place[4 + n] = jnp.where(r == target_i, 1.0, 0.0).astype(BF16)
        return carry

    lax.fori_loop(0, 2, lay_body, 0)

    for now in range(STEPS):
        final = now == STEPS - 1
        f = field.at[now]

        blend = jnp.zeros((rows, LANES), F32)
        for first, count, plane in GROUPS:
            for part in range(count // 8):
                high, low = split(f[first + 8 * part : first + 8 * part + 8].reshape(LANES, LANES))
                n = plane // 8 + part
                both = dot(w_high[n], jnp.concatenate([high, low], axis=1))
                blend += both[:, :LANES] + both[:, LANES:] + dot(w_low[n], high)

        for copy in halo_copies(now):
            copy.wait_recv()

        zero = jnp.zeros((Z, LANES), F32)
        f[0] = jnp.where(q == 0, zero, f[0])
        f[33] = jnp.where(q == nx - 1, zero, f[33])
        in_back = lane < 63
        below = jnp.where((j == 0) & (in_back | (lane == 127)), zero, edge_below[now])
        above = jnp.where((j == ny - 1) & in_back, zero, edge_above[now])
        even = lane % 2 == 0
        edges = jnp.where(even, above, below)
        corner = edge_corner[now]
        corner_back = jnp.where((j == ny - 1) | (q == nx - 1), zero, corner)
        high_y = jnp.where(even, above, zero)
        high_y = jnp.where(lane == 1, pltpu.roll(corner_back, 1, 1), high_y)
        high_y = jnp.where(lane == 3, pltpu.roll(corner, LANES - 61, 1), high_y)
        high_y = jnp.where(lane == 5, pltpu.roll(corner, LANES - 91, 1), high_y)

        beyond_x = jnp.concatenate([f[33], f[51], f[69]], axis=0)
        blend += exact_dot(w_halo[:, 0:48], beyond_x)
        high_y = jnp.concatenate([high_y, jnp.zeros((LANES - Z, LANES), F32)], axis=0)
        spill = exact_dot(w_x[...], high_y, ((1,), (1,)))
        spill = jnp.sum(w_z[...] * spill, axis=1, keepdims=True)
        ahead = pltpu.roll(blend, LANES - 1, 1)
        ahead = jnp.where(iota((rows, LANES), 1) == LANES - 1, spill, ahead)
        mixed = blend + share_y[...] * (ahead - blend)
        sent[now] = mixed.reshape(64, 4, LANES)

        def send(step, carry):
            to = lax.rem(q + step, nx)
            pltpu.make_async_remote_copy(
                src_ref=sent.at[now, to],
                dst_ref=got.at[now, q],
                send_sem=swap_send.at[now],
                recv_sem=swap_recv.at[now],
                device_id={"gx": to},
                device_id_type=MESH,
            ).start()
            return carry

        lax.fori_loop(1, nx, send, 0)
        got[now, pl.ds(q, 1)] = sent[now, pl.ds(q, 1)]

        for first, count, plane in GROUPS:
            a, b, c, d = BACK if count == 32 else BODY
            layers = iota((Z, LANES), 0)

            def step_plane(n, carry, first=first, plane=plane, a=a, b=b, c=c, d=d):
                here = f[first + n]
                side = pltpu.roll(edges, LANES - 2 * (plane + n), 1)
                back_y = pltpu.roll(jnp.where(lane == LANES - 1, side, here), 1, 1)
                ahead_y = pltpu.roll(jnp.where(lane == 0, side, here), LANES - 1, 1)
                back_z = jnp.where(layers == 0, 0.0, pltpu.roll(here, 1, 0))
                ahead_z = jnp.where(layers == Z - 1, 0.0, pltpu.roll(here, Z - 1, 0))
                new = (
                    (1.0 - a - b - c - 6.0 * d) * here
                    + (a + d) * f[first + n - 1]
                    + d * f[first + n + 1]
                    + (b + d) * back_y
                    + d * ahead_y
                    + (c + d) * back_z
                    + d * ahead_z
                )
                if plane == 0:
                    new = new * keep[n // 8, pl.ds(pl.multiple_of(n % 8 * Z, Z), Z)]
                else:
                    new = jnp.where(layers >= Z - 2, 0.0, new)
                moved[plane + n] = new
                return carry

            for n in range(count):
                step_plane(n, 0)

        pltpu.make_async_remote_copy(
            src_ref=sent.at[now, pl.ds(0, nx - 1)],
            dst_ref=got.at[now, pl.ds(0, nx - 1)],
            send_sem=swap_send.at[now],
            recv_sem=swap_recv.at[now],
            device_id={"gx": q_up},
            device_id_type=MESH,
        ).wait_recv()

        high, low = split(got[now].reshape(rows, LANES))
        received = jnp.concatenate([high, low], axis=1)
        for n in range(6):
            both = dot(place[n], received)
            added = both[:, :LANES] + both[:, LANES:]
            if n < 4:
                new = moved[8 * n : 8 * n + 8] + added.reshape(8, Z, LANES)
                if final:
                    back_out[8 * n : 8 * n + 8] = new
                else:
                    field[now + 1, 1 + 8 * n : 9 + 8 * n] = new
            else:
                start = 32 + 16 * (n - 4)
                low_part = moved[start : start + 16, 0:8]
                new = moved[start : start + 16, 8:16] + added.reshape(16, 8, LANES)
                if final:
                    body_out[n - 4, :, 0:8] = low_part
                    body_out[n - 4, :, 8:16] = new
                else:
                    first = GROUPS[n - 3][0]
                    field[now + 1, first : first + 16, 0:8] = low_part
                    field[now + 1, first : first + 16, 8:16] = new
        if not final:
            pack_edges(now + 1)
            for copy in halo_copies(now + 1):
                copy.start()

    for now in range(STEPS):
        for copy in halo_copies(now):
            copy.wait_send()
        pltpu.make_async_remote_copy(
            src_ref=sent.at[now, pl.ds(0, nx - 1)],
            dst_ref=got.at[now, pl.ds(0, nx - 1)],
            send_sem=swap_send.at[now],
            recv_sem=swap_recv.at[now],
            device_id={"gx": q_up},
            device_id_type=MESH,
        ).wait_send()


def per_device(
    background,
    nearbody,
    donor_rows,
    donor_fractions,
    fringe_slots,
    return_rows,
    return_fractions,
    hole_slots,
):
    nx, ny = lax.axis_size("gx"), lax.axis_size("gy")
    by_slot = lambda rows: jnp.swapaxes(rows[0, 0], 0, 1)
    shares = lambda parts: jnp.swapaxes(parts[:, 0, 0], 1, 2)
    vmem = pl.BlockSpec(memory_space=pltpu.VMEM)
    hbm = pl.BlockSpec(memory_space=pl.ANY)
    dma = pltpu.SemaphoreType.DMA
    return pl.pallas_call(
        functools.partial(kernel, nx, ny),
        out_shape=(
            jax.ShapeDtypeStruct(background.shape, F32),
            jax.ShapeDtypeStruct(nearbody.shape, F32),
        ),
        in_specs=[hbm, hbm] + [vmem] * 6,
        out_specs=(vmem, vmem),
        scratch_shapes=[
            pltpu.VMEM((STEPS, PLANES, Z, LANES), F32),
            pltpu.VMEM((64, Z, LANES), F32),
            pltpu.VMEM((24, LANES), F32),
            pltpu.VMEM((8, 256, LANES), BF16),
            pltpu.VMEM((8, 256, LANES), BF16),
            pltpu.VMEM((256, LANES), F32),
            pltpu.VMEM((256, LANES), F32),
            pltpu.VMEM((256, LANES), F32),
            pltpu.VMEM((256, LANES), F32),
            pltpu.VMEM((6, LANES, 256), BF16),
            pltpu.VMEM((4, LANES, LANES), F32),
            pltpu.VMEM((STEPS, Z, LANES), F32),
            pltpu.VMEM((STEPS, Z, LANES), F32),
            pltpu.VMEM((STEPS, Z, LANES), F32),
            pltpu.VMEM((STEPS, Z, LANES), F32),
            pltpu.VMEM((STEPS, 64, 4, LANES), F32),
            pltpu.VMEM((STEPS, 64, 4, LANES), F32),
            dma((3,)),
            dma((STEPS, 9)),
            dma((STEPS, 9)),
            dma((STEPS,)),
            dma((STEPS,)),
            dma((3,)),
        ],
        compiler_params=pltpu.CompilerParams(
            collective_id=0, has_side_effects=True, vmem_limit_bytes=32 * 1024 * 1024
        ),
        name="overset_steps",
    )(
        background,
        nearbody,
        by_slot(donor_rows),
        shares(donor_fractions),
        by_slot(fringe_slots),
        by_slot(return_rows),
        shares(return_fractions),
        by_slot(hole_slots),
    )


def solution(mesh):
    placed = (
        P("gx", None, "gy"),
        P(None, "gx", None, "gy"),
        P("gx", "gy", None, None),
        P(None, "gx", "gy", None, None),
        P("gx", "gy", None, None),
        P("gx", "gy", None, None),
        P(None, "gx", "gy", None, None),
        P("gx", "gy", None, None),
    )
    return jax.shard_map(
        per_device,
        mesh=mesh,
        in_specs=placed,
        out_specs=(P("gx", None, "gy"), P(None, "gx", None, "gy")),
        check_vma=False,
    )
```

```python
import functools

import jax
import jax.numpy as jnp
from jax import lax
from jax.experimental import pallas as pl
from jax.experimental.pallas import tpu as pltpu
from jax.sharding import PartitionSpec as P

STEPS = 2
MESH = pl.DeviceIdType.MESH

BACK = (0.3, 0.25, 0.15, 0.04)
BODY = (0.2, 0.3, 0.2, 0.045)

GROUPS = ((1, 32, 0), (35, 16, 32), (53, 16, 48))
PLANES = 70
Z = 16
LANES = 128
F32 = jnp.float32
BF16 = jnp.bfloat16


def iota(shape, dim):
    return lax.broadcasted_iota(jnp.int32, shape, dim)


def split(value):
    high = value.astype(BF16)
    return high, (value - high.astype(F32)).astype(BF16)


def dot(a, b):
    return jnp.dot(a, b, preferred_element_type=F32)


def exact_dot(a, b, dims=((1,), (0,))):
    return lax.dot_general(
        a, b, (dims, ((), ())), precision=lax.Precision.HIGHEST, preferred_element_type=F32
    )


def peer(q, step):
    def away(n):
        return 4 + (1 - 2 * (n % 2)) * ((n + 1) // 2)

    return (q // 8 + away(step // 8)) % 8 * 8 + (q % 8 + away(step % 8)) % 8


def kernel(
    nx,
    ny,
    back_ref,
    body_ref,
    donor_rows_ref,
    donor_fractions_ref,
    fringe_slots_ref,
    return_rows_ref,
    return_fractions_ref,
    hole_slots_ref,
    back_out,
    body_out,
    donor_rows,
    donor_fractions,
    fringe_slots,
    return_rows,
    return_fractions,
    hole_slots,
    field,
    moved,
    table,
    w_high,
    w_low,
    w_halo,
    w_x,
    w_z,
    share_y,
    place,
    keep,
    edge,
    edge_above,
    edge_below,
    edge_corner,
    sent,
    got,
    in_sem,
    halo_send,
    halo_recv,
    swap_send,
    swap_recv,
):
    q = lax.axis_index("gx")
    j = lax.axis_index("gy")
    q_up, q_down = lax.rem(q + 1, nx), lax.rem(q + nx - 1, nx)
    j_up, j_down = lax.rem(j + 1, ny), lax.rem(j + ny - 1, ny)

    loads = [
        pltpu.make_async_copy(back_ref, field.at[0, pl.ds(1, 32)], in_sem.at[0]),
        pltpu.make_async_copy(body_ref.at[0], field.at[0, pl.ds(35, 16)], in_sem.at[1]),
        pltpu.make_async_copy(body_ref.at[1], field.at[0, pl.ds(53, 16)], in_sem.at[2]),
    ]
    tables = [
        pltpu.make_async_copy(src, dst, in_sem.at[3 + n])
        for n, (src, dst) in enumerate(
            (
                (donor_rows_ref, donor_rows),
                (donor_fractions_ref, donor_fractions),
                (fringe_slots_ref, fringe_slots),
                (return_rows_ref, return_rows),
                (return_fractions_ref, return_fractions),
                (hole_slots_ref, hole_slots),
            )
        )
    ]
    for load in loads + tables:
        load.start()

    barrier = pltpu.get_barrier_semaphore()

    def greet(step, carry):
        pl.semaphore_signal(barrier, inc=1, device_id={"gx": peer(q, step)}, device_id_type=MESH)
        return carry

    lax.fori_loop(0, nx - 1, greet, 0, unroll=True)
    for there in ((q, j_up), (q, j_down), (q_down, j_down), (q_up, j_up)):
        pl.semaphore_signal(
            barrier, inc=1, device_id={"gx": there[0], "gy": there[1]}, device_id_type=MESH
        )

    def halo_copies(now):
        f = field.at[now]
        pairs = []
        for n, (first, count, _) in enumerate(GROUPS):
            pairs.append((f.at[first + count - 1], f.at[first - 1], q_up, j))
            pairs.append((f.at[first], f.at[first + count], q_down, j))
        pairs.append((edge.at[now], edge_below.at[now], q, j_up))
        pairs.append((edge.at[now], edge_above.at[now], q, j_down))
        pairs.append((edge.at[now], edge_corner.at[now], q_down, j_down))
        return [
            pltpu.make_async_remote_copy(
                src_ref=src,
                dst_ref=dst,
                send_sem=halo_send.at[now, n],
                recv_sem=halo_recv.at[now, n],
                device_id={"gx": to_q, "gy": to_j},
                device_id_type=MESH,
            )
            for n, (src, dst, to_q, to_j) in enumerate(pairs)
        ]

    lane = iota((Z, LANES), 1)

    def pack_edges(now):
        packed = jnp.zeros((Z, LANES), F32)
        for first, count, plane in GROUPS:
            for k in range(count):
                spot = 2 * (plane + k)
                rolled = pltpu.roll(field[now, first + k], spot, 1)
                hit = (lane == spot) | (lane == (spot - 1) % LANES)
                packed = jnp.where(hit, rolled, packed)
        edge[now] = packed

    for load in tables:
        load.wait()
    table[...] = jnp.zeros_like(table)
    half = ((donor_rows, return_rows), (fringe_slots, hole_slots))
    for n, (first, second) in enumerate(half):
        table[4 * n : 4 * n + 2, 0:64] = first[...].astype(F32)
        table[4 * n + 2 : 4 * n + 4, 0:64] = second[...].astype(F32)
    for n in range(3):
        table[8 + 4 * n : 10 + 4 * n, 0:64] = donor_fractions[n]
        table[10 + 4 * n : 12 + 4 * n, 0:64] = return_fractions[n]
    rows = 4 * 64
    spread = (iota((LANES, rows), 1) // 4 == iota((LANES, rows), 0)).astype(F32)
    wide = exact_dot(table[...], spread)
    kind = iota((1, rows), 1) % 4

    def pick(n):
        x = wide[4 * n : 4 * n + 4]
        return jnp.where(
            kind == 0, x[0:1], jnp.where(kind == 1, x[1:2], jnp.where(kind == 2, x[2:3], x[3:4]))
        )

    row = jnp.maximum(pick(0), 0.0)
    slot = pick(1)
    donor = kind < 2
    used = jnp.where(donor, float(Z - 1), float(Z - 3))
    plane = jnp.floor((row + 0.5) / used)
    layer = row - plane * used
    plane = jnp.where(donor, plane, plane + 32.0)
    target = jnp.where(slot < 0.0, -1.0, jnp.where(donor, slot + 512.0, slot))
    columns = jnp.concatenate(
        [plane, layer, pick(2), pick(3), pick(4), jnp.zeros((3, rows), F32)], axis=0
    ).T
    plane_c = columns[:, 0:1].astype(jnp.int32)
    layer_c = columns[:, 1:2].astype(jnp.int32)
    f1, f2, f3 = columns[:, 2:3], columns[:, 3:4], columns[:, 4:5]
    share_y[...] = jnp.broadcast_to(f3, (rows, LANES))
    last = (plane_c == 31) | (plane_c == 47) | (plane_c == 63)
    halo_index = jnp.where(plane_c == 31, 0, jnp.where(plane_c == 47, 1, 2))
    w00, w01 = (1.0 - f1) * (1.0 - f2), (1.0 - f1) * f2
    w10, w11 = f1 * (1.0 - f2), f1 * f2
    base = plane_c * Z + layer_c
    far = jnp.where(last, -1000, base + Z)

    def weigh(n, carry):
        k = iota((rows, LANES), 1) + n * LANES
        w = (
            jnp.where(k == base, w00, 0.0)
            + jnp.where(k == base + 1, w01, 0.0)
            + jnp.where(k == far, w10, 0.0)
            + jnp.where(k == far + 1, w11, 0.0)
        )
        high, low = split(w)
        w_high[n] = high
        w_low[n] = low
        return carry

    lax.fori_loop(0, 8, weigh, 0)
    k = iota((rows, LANES), 1)
    near = jnp.where(last, halo_index * Z + layer_c, -1000)
    w_halo[...] = jnp.where(k == near, w10, 0.0) + jnp.where(k == near + 1, w11, 0.0)
    beyond = jnp.where(last, 1 + 2 * halo_index, 2 * plane_c + 2)
    w_x[...] = jnp.where(k == 2 * plane_c, 1.0 - f1, 0.0) + jnp.where(k == beyond, f1, 0.0)
    w_z[...] = jnp.where(k == layer_c, 1.0 - f2, 0.0) + jnp.where(k == layer_c + 1, f2, 0.0)

    target_i = target.astype(jnp.int32)
    ones = jnp.ones((rows, LANES), BF16)

    def lay_back(n, carry):
        r = iota((LANES, rows), 0) + n * LANES
        hit = jnp.where(r == target_i, 1.0, 0.0).astype(BF16)
        place[n] = hit
        keep[n] = 1.0 - dot(hit, ones)
        return carry

    lax.fori_loop(0, 4, lay_back, 0)

    def lay_body(n, carry):
        r = iota((LANES, rows), 0)
        r = 512 + (r // 8 + n * 16) * Z + 8 + r % 8
        place[4 + n] = jnp.where(r == target_i, 1.0, 0.0).astype(BF16)
        return carry

    lax.fori_loop(0, 2, lay_body, 0)

    for load in loads:
        load.wait()
    pack_edges(0)
    pl.semaphore_wait(barrier, nx - 1 + 4)
    for copy in halo_copies(0):
        copy.start()

    for now in range(STEPS):
        final = now == STEPS - 1
        f = field.at[now]

        blend = jnp.zeros((rows, LANES), F32)
        for first, count, plane in GROUPS:
            for part in range(count // 8):
                high, low = split(f[first + 8 * part : first + 8 * part + 8].reshape(LANES, LANES))
                n = plane // 8 + part
                both = dot(w_high[n], jnp.concatenate([high, low], axis=1))
                blend += both[:, :LANES] + both[:, LANES:] + dot(w_low[n], high)

        for copy in halo_copies(now):
            copy.wait_recv()

        zero = jnp.zeros((Z, LANES), F32)
        f[0] = jnp.where(q == 0, zero, f[0])
        f[33] = jnp.where(q == nx - 1, zero, f[33])
        in_back = lane < 63
        below = jnp.where((j == 0) & (in_back | (lane == 127)), zero, edge_below[now])
        above = jnp.where((j == ny - 1) & in_back, zero, edge_above[now])
        even = lane % 2 == 0
        edges = jnp.where(even, above, below)
        corner = edge_corner[now]
        corner_back = jnp.where((j == ny - 1) | (q == nx - 1), zero, corner)
        high_y = jnp.where(even, above, zero)
        high_y = jnp.where(lane == 1, pltpu.roll(corner_back, 1, 1), high_y)
        high_y = jnp.where(lane == 3, pltpu.roll(corner, LANES - 61, 1), high_y)
        high_y = jnp.where(lane == 5, pltpu.roll(corner, LANES - 91, 1), high_y)

        beyond_x = jnp.concatenate([f[33], f[51], f[69]], axis=0)
        blend += exact_dot(w_halo[:, 0:48], beyond_x)
        high_y = jnp.concatenate([high_y, jnp.zeros((LANES - Z, LANES), F32)], axis=0)
        spill = exact_dot(w_x[...], high_y, ((1,), (1,)))
        spill = jnp.sum(w_z[...] * spill, axis=1, keepdims=True)
        ahead = pltpu.roll(blend, LANES - 1, 1)
        ahead = jnp.where(iota((rows, LANES), 1) == LANES - 1, spill, ahead)
        mixed = blend + share_y[...] * (ahead - blend)
        sent[now] = mixed.reshape(64, 4, LANES)

        def send(step, carry):
            to = peer(q, step)
            pltpu.make_async_remote_copy(
                src_ref=sent.at[now, to],
                dst_ref=got.at[now, q],
                send_sem=swap_send.at[now],
                recv_sem=swap_recv.at[now],
                device_id={"gx": to},
                device_id_type=MESH,
            ).start()
            return carry

        lax.fori_loop(0, nx - 1, send, 0, unroll=True)
        got[now, pl.ds(q, 1)] = sent[now, pl.ds(q, 1)]

        for first, count, plane in GROUPS:
            a, b, c, d = BACK if count == 32 else BODY
            layers = iota((Z, LANES), 0)

            def step_plane(n, carry, first=first, plane=plane, a=a, b=b, c=c, d=d):
                here = f[first + n]
                side = pltpu.roll(edges, LANES - 2 * (plane + n), 1)
                back_y = pltpu.roll(jnp.where(lane == LANES - 1, side, here), 1, 1)
                ahead_y = pltpu.roll(jnp.where(lane == 0, side, here), LANES - 1, 1)
                back_z = jnp.where(layers == 0, 0.0, pltpu.roll(here, 1, 0))
                ahead_z = jnp.where(layers == Z - 1, 0.0, pltpu.roll(here, Z - 1, 0))
                new = (
                    (1.0 - a - b - c - 6.0 * d) * here
                    + (a + d) * f[first + n - 1]
                    + d * f[first + n + 1]
                    + (b + d) * back_y
                    + d * ahead_y
                    + (c + d) * back_z
                    + d * ahead_z
                )
                if plane == 0:
                    new = new * keep[n // 8, pl.ds(pl.multiple_of(n % 8 * Z, Z), Z)]
                else:
                    new = jnp.where(layers >= Z - 2, 0.0, new)
                moved[plane + n] = new
                return carry

            for n in range(count):
                step_plane(n, 0)

        pltpu.make_async_remote_copy(
            src_ref=sent.at[now, pl.ds(0, nx - 1)],
            dst_ref=got.at[now, pl.ds(0, nx - 1)],
            send_sem=swap_send.at[now],
            recv_sem=swap_recv.at[now],
            device_id={"gx": q_up},
            device_id_type=MESH,
        ).wait_recv()

        high, low = split(got[now].reshape(rows, LANES))
        received = jnp.concatenate([high, low], axis=1)
        for n in range(6):
            both = dot(place[n], received)
            added = both[:, :LANES] + both[:, LANES:]
            if n < 4:
                new = moved[8 * n : 8 * n + 8] + added.reshape(8, Z, LANES)
                if final:
                    back_out[8 * n : 8 * n + 8] = new
                else:
                    field[now + 1, 1 + 8 * n : 9 + 8 * n] = new
            else:
                start = 32 + 16 * (n - 4)
                low_part = moved[start : start + 16, 0:8]
                new = moved[start : start + 16, 8:16] + added.reshape(16, 8, LANES)
                if final:
                    body_out[n - 4, :, 0:8] = low_part
                    body_out[n - 4, :, 8:16] = new
                else:
                    first = GROUPS[n - 3][0]
                    field[now + 1, first : first + 16, 0:8] = low_part
                    field[now + 1, first : first + 16, 8:16] = new
        if not final:
            pack_edges(now + 1)
            for copy in halo_copies(now + 1):
                copy.start()

    for now in range(STEPS):
        for copy in halo_copies(now):
            copy.wait_send()
        pltpu.make_async_remote_copy(
            src_ref=sent.at[now, pl.ds(0, nx - 1)],
            dst_ref=got.at[now, pl.ds(0, nx - 1)],
            send_sem=swap_send.at[now],
            recv_sem=swap_recv.at[now],
            device_id={"gx": q_up},
            device_id_type=MESH,
        ).wait_send()


def per_device(
    background,
    nearbody,
    donor_rows,
    donor_fractions,
    fringe_slots,
    return_rows,
    return_fractions,
    hole_slots,
):
    nx, ny = lax.axis_size("gx"), lax.axis_size("gy")
    by_slot = lambda rows: jnp.swapaxes(rows[0, 0], 0, 1)
    shares = lambda parts: jnp.swapaxes(parts[:, 0, 0], 1, 2)
    vmem = pl.BlockSpec(memory_space=pltpu.VMEM)
    hbm = pl.BlockSpec(memory_space=pltpu.HBM)
    dma = pltpu.SemaphoreType.DMA
    return pl.pallas_call(
        functools.partial(kernel, nx, ny),
        out_shape=(
            jax.ShapeDtypeStruct(background.shape, F32),
            jax.ShapeDtypeStruct(nearbody.shape, F32),
        ),
        in_specs=[hbm] * 8,
        out_specs=(vmem, vmem),
        scratch_shapes=[
            pltpu.VMEM((2, 64), jnp.int32),
            pltpu.VMEM((3, 2, 64), F32),
            pltpu.VMEM((2, 64), jnp.int32),
            pltpu.VMEM((2, 64), jnp.int32),
            pltpu.VMEM((3, 2, 64), F32),
            pltpu.VMEM((2, 64), jnp.int32),
            pltpu.VMEM((STEPS, PLANES, Z, LANES), F32),
            pltpu.VMEM((64, Z, LANES), F32),
            pltpu.VMEM((24, LANES), F32),
            pltpu.VMEM((8, 256, LANES), BF16),
            pltpu.VMEM((8, 256, LANES), BF16),
            pltpu.VMEM((256, LANES), F32),
            pltpu.VMEM((256, LANES), F32),
            pltpu.VMEM((256, LANES), F32),
            pltpu.VMEM((256, LANES), F32),
            pltpu.VMEM((6, LANES, 256), BF16),
            pltpu.VMEM((4, LANES, LANES), F32),
            pltpu.VMEM((STEPS, Z, LANES), F32),
            pltpu.VMEM((STEPS, Z, LANES), F32),
            pltpu.VMEM((STEPS, Z, LANES), F32),
            pltpu.VMEM((STEPS, Z, LANES), F32),
            pltpu.VMEM((STEPS, 64, 4, LANES), F32),
            pltpu.VMEM((STEPS, 64, 4, LANES), F32),
            dma((9,)),
            dma((STEPS, 9)),
            dma((STEPS, 9)),
            dma((STEPS,)),
            dma((STEPS,)),
        ],
        compiler_params=pltpu.CompilerParams(
            collective_id=0, has_side_effects=True, vmem_limit_bytes=32 * 1024 * 1024
        ),
        name="overset_steps",
    )(
        *(
            pltpu.with_memory_space_constraint(operand, pltpu.HBM)
            for operand in (
                background,
                nearbody,
                by_slot(donor_rows),
                shares(donor_fractions),
                by_slot(fringe_slots),
                by_slot(return_rows),
                shares(return_fractions),
                by_slot(hole_slots),
            )
        )
    )


def solution(mesh):
    placed = (
        P("gx", None, "gy"),
        P(None, "gx", None, "gy"),
        P("gx", "gy", None, None),
        P(None, "gx", "gy", None, None),
        P("gx", "gy", None, None),
        P("gx", "gy", None, None),
        P(None, "gx", "gy", None, None),
        P("gx", "gy", None, None),
    )
    return jax.shard_map(
        per_device,
        mesh=mesh,
        in_specs=placed,
        out_specs=(P("gx", None, "gy"), P(None, "gx", None, "gy")),
        check_vma=False,
    )
```

```python
import functools

import jax
import jax.numpy as jnp
from jax import lax
from jax.experimental import pallas as pl
from jax.experimental.pallas import tpu as pltpu
from jax.sharding import PartitionSpec as P

STEPS = 2
MESH = pl.DeviceIdType.MESH

BACK = (0.3, 0.25, 0.15, 0.04)
BODY = (0.2, 0.3, 0.2, 0.045)

GROUPS = ((1, 32, 0), (35, 16, 32), (53, 16, 48))
PLANES = 70
Z = 16
LANES = 128
F32 = jnp.float32
BF16 = jnp.bfloat16


def iota(shape, dim):
    return lax.broadcasted_iota(jnp.int32, shape, dim)


def split(value):
    high = value.astype(BF16)
    return high, (value - high.astype(F32)).astype(BF16)


def dot(a, b):
    return jnp.dot(a, b, preferred_element_type=F32)


def exact_dot(a, b, dims=((1,), (0,))):
    return lax.dot_general(
        a, b, (dims, ((), ())), precision=lax.Precision.HIGHEST, preferred_element_type=F32
    )


def peer(q, step):
    def away(n):
        return 4 + (1 - 2 * (n % 2)) * ((n + 1) // 2)

    return (q // 8 + away(step // 8)) % 8 * 8 + (q % 8 + away(step % 8)) % 8


def kernel(
    nx,
    ny,
    back_ref,
    body_ref,
    donor_rows_ref,
    donor_fractions_ref,
    fringe_slots_ref,
    return_rows_ref,
    return_fractions_ref,
    hole_slots_ref,
    back_out,
    body_out,
    donor_rows,
    donor_fractions,
    fringe_slots,
    return_rows,
    return_fractions,
    hole_slots,
    field,
    moved,
    table,
    w_high,
    w_low,
    w_halo,
    w_x,
    w_z,
    share_y,
    place,
    keep,
    edge,
    corner,
    edge_above,
    edge_below,
    edge_corner,
    sent,
    got,
    in_sem,
    halo_send,
    halo_recv,
    swap_send,
    swap_recv,
):
    q = lax.axis_index("gx")
    j = lax.axis_index("gy")
    q_up, q_down = lax.rem(q + 1, nx), lax.rem(q + nx - 1, nx)
    j_up, j_down = lax.rem(j + 1, ny), lax.rem(j + ny - 1, ny)

    loads = [
        pltpu.make_async_copy(back_ref, field.at[0, pl.ds(1, 32)], in_sem.at[0]),
        pltpu.make_async_copy(body_ref.at[0], field.at[0, pl.ds(35, 16)], in_sem.at[1]),
        pltpu.make_async_copy(body_ref.at[1], field.at[0, pl.ds(53, 16)], in_sem.at[2]),
    ]
    tables = [
        pltpu.make_async_copy(src, dst, in_sem.at[3 + n])
        for n, (src, dst) in enumerate(
            (
                (donor_rows_ref, donor_rows),
                (donor_fractions_ref, donor_fractions),
                (fringe_slots_ref, fringe_slots),
                (return_rows_ref, return_rows),
                (return_fractions_ref, return_fractions),
                (hole_slots_ref, hole_slots),
            )
        )
    ]
    for load in loads + tables:
        load.start()

    barrier = pltpu.get_barrier_semaphore()

    def greet(step, carry):
        pl.semaphore_signal(barrier, inc=1, device_id={"gx": peer(q, step)}, device_id_type=MESH)
        return carry

    lax.fori_loop(0, nx - 1, greet, 0, unroll=True)
    for there in ((q, j_up), (q, j_down), (q_down, j_down), (q_up, j_up)):
        pl.semaphore_signal(
            barrier, inc=1, device_id={"gx": there[0], "gy": there[1]}, device_id_type=MESH
        )

    def halo_copies(now, which=range(9)):
        f = field.at[now]
        pairs = []
        for n, (first, count, _) in enumerate(GROUPS):
            pairs.append((f.at[first + count - 1], f.at[first - 1], q_up, j))
            pairs.append((f.at[first], f.at[first + count], q_down, j))
        pairs.append((edge.at[now], edge_below.at[now], q, j_up))
        pairs.append((edge.at[now], edge_above.at[now], q, j_down))
        pairs.append((corner.at[now], edge_corner.at[now], q_down, j_down))
        return [
            pltpu.make_async_remote_copy(
                src_ref=src,
                dst_ref=dst,
                send_sem=halo_send.at[now, n],
                recv_sem=halo_recv.at[now, n],
                device_id={"gx": to_q, "gy": to_j},
                device_id_type=MESH,
            )
            for n in which
            for src, dst, to_q, to_j in pairs[n : n + 1]
        ]

    lane = iota((Z, LANES), 1)

    def pack_edges(now):
        packed = jnp.zeros((Z, LANES), F32)
        for first, count, plane in GROUPS:
            for k in range(count):
                spot = 2 * (plane + k)
                rolled = pltpu.roll(field[now, first + k], spot, 1)
                hit = (lane == spot) | (lane == (spot - 1) % LANES)
                packed = jnp.where(hit, rolled, packed)
        edge[now] = packed

    def pack_corner(now):
        packed = jnp.zeros((Z, LANES), F32)
        for n, (first, _, _) in enumerate(GROUPS):
            spot = 2 * n + 1
            packed = jnp.where(lane == spot, pltpu.roll(field[now, first], spot, 1), packed)
        corner[now] = packed

    def start_halos(now, which):
        for copy in halo_copies(now, which):
            copy.start()

    for load in tables:
        load.wait()
    table[...] = jnp.zeros_like(table)
    half = ((donor_rows, return_rows), (fringe_slots, hole_slots))
    for n, (first, second) in enumerate(half):
        table[4 * n : 4 * n + 2, 0:64] = first[...].astype(F32)
        table[4 * n + 2 : 4 * n + 4, 0:64] = second[...].astype(F32)
    for n in range(3):
        table[8 + 4 * n : 10 + 4 * n, 0:64] = donor_fractions[n]
        table[10 + 4 * n : 12 + 4 * n, 0:64] = return_fractions[n]
    rows = 4 * 64
    spread = (iota((LANES, rows), 1) // 4 == iota((LANES, rows), 0)).astype(F32)
    wide = exact_dot(table[...], spread)
    kind = iota((1, rows), 1) % 4

    def pick(n):
        x = wide[4 * n : 4 * n + 4]
        return jnp.where(
            kind == 0, x[0:1], jnp.where(kind == 1, x[1:2], jnp.where(kind == 2, x[2:3], x[3:4]))
        )

    row = jnp.maximum(pick(0), 0.0)
    slot = pick(1)
    donor = kind < 2
    used = jnp.where(donor, float(Z - 1), float(Z - 3))
    plane = jnp.floor((row + 0.5) / used)
    layer = row - plane * used
    plane = jnp.where(donor, plane, plane + 32.0)
    target = jnp.where(slot < 0.0, -1.0, jnp.where(donor, slot + 512.0, slot))
    columns = jnp.concatenate(
        [plane, layer, pick(2), pick(3), pick(4), jnp.zeros((3, rows), F32)], axis=0
    ).T
    plane_c = columns[:, 0:1].astype(jnp.int32)
    layer_c = columns[:, 1:2].astype(jnp.int32)
    f1, f2, f3 = columns[:, 2:3], columns[:, 3:4], columns[:, 4:5]
    share_y[...] = jnp.broadcast_to(f3, (rows, LANES))
    last = (plane_c == 31) | (plane_c == 47) | (plane_c == 63)
    halo_index = jnp.where(plane_c == 31, 0, jnp.where(plane_c == 47, 1, 2))
    w00, w01 = (1.0 - f1) * (1.0 - f2), (1.0 - f1) * f2
    w10, w11 = f1 * (1.0 - f2), f1 * f2
    base = plane_c * Z + layer_c
    far = jnp.where(last, -1000, base + Z)

    def weigh(n, carry):
        k = iota((rows, 2 * LANES), 1) + n * (2 * LANES)
        w = (
            jnp.where(k == base, w00, 0.0)
            + jnp.where(k == base + 1, w01, 0.0)
            + jnp.where(k == far, w10, 0.0)
            + jnp.where(k == far + 1, w11, 0.0)
        )
        high, low = split(w)
        w_high[n] = high
        w_low[n] = low
        return carry

    lax.fori_loop(0, 4, weigh, 0)
    k = iota((rows, LANES), 1)
    near = jnp.where(last, halo_index * Z + layer_c, -1000)
    high, low = split(jnp.where(k == near, w10, 0.0) + jnp.where(k == near + 1, w11, 0.0))
    w_halo[0] = high
    w_halo[1] = low
    beyond = jnp.where(last, 1 + 2 * halo_index, 2 * plane_c + 2)
    high, low = split(
        jnp.where(k == 2 * plane_c, 1.0 - f1, 0.0) + jnp.where(k == beyond, f1, 0.0)
    )
    w_x[...] = jnp.concatenate([high, low], axis=1)
    k = jnp.where(k < 2 * Z, k % Z, -1000)
    w_z[...] = jnp.where(k == layer_c, 1.0 - f2, 0.0) + jnp.where(k == layer_c + 1, f2, 0.0)

    target_i = target.astype(jnp.int32)
    ones = jnp.ones((rows, LANES), BF16)

    def lay_back(n, carry):
        r = iota((LANES, rows), 0) + n * LANES
        hit = jnp.where(r == target_i, 1.0, 0.0).astype(BF16)
        place[n] = hit
        keep[n] = 1.0 - dot(hit, ones)
        return carry

    lax.fori_loop(0, 4, lay_back, 0)

    def lay_body(n, carry):
        r = iota((LANES, rows), 0)
        r = 512 + (r // 8 + n * 16) * Z + 8 + r % 8
        place[4 + n] = jnp.where(r == target_i, 1.0, 0.0).astype(BF16)
        return carry

    lax.fori_loop(0, 2, lay_body, 0)

    for load in loads:
        load.wait()
    pack_corner(0)
    pack_edges(0)
    pl.semaphore_wait(barrier, nx - 1 + 4)
    start_halos(0, (8, 1, 3, 5, 0, 2, 4, 6, 7))

    for now in range(STEPS):
        final = now == STEPS - 1
        f = field.at[now]

        blend = jnp.zeros((rows, LANES), F32)
        for first, count, plane in GROUPS:
            for part in range(count // 16):
                start = first + 16 * part
                high, low = split(f[start : start + 16].reshape(2 * LANES, LANES))
                n = plane // 16 + part
                both = dot(w_high[n], jnp.concatenate([high, low], axis=1))
                blend += both[:, :LANES] + both[:, LANES:] + dot(w_low[n], high)

        for copy in halo_copies(now):
            copy.wait_recv()

        zero = jnp.zeros((Z, LANES), F32)
        f[0] = jnp.where(q == 0, zero, f[0])
        f[33] = jnp.where(q == nx - 1, zero, f[33])
        in_back = lane < 63
        below = jnp.where((j == 0) & (in_back | (lane == 127)), zero, edge_below[now])
        above = jnp.where((j == ny - 1) & in_back, zero, edge_above[now])
        even = lane % 2 == 0
        edges = jnp.where(even, above, below)
        ends = (lane == 1) & ((j == ny - 1) | (q == nx - 1))
        high, low = split(jnp.where(even, above, jnp.where(ends, zero, edge_corner[now])))
        high_y = jnp.concatenate(
            [
                jnp.concatenate([high, high], axis=1),
                jnp.concatenate([low, jnp.zeros((Z, LANES), BF16)], axis=1),
                jnp.zeros((LANES - 2 * Z, 2 * LANES), BF16),
            ],
            axis=0,
        )
        spill = lax.dot_general(
            w_x[...], high_y, (((1,), (1,)), ((), ())), preferred_element_type=F32
        )

        high, low = split(jnp.concatenate([f[33], f[51], f[69]], axis=0))
        both = dot(w_halo[0, :, 0:48], jnp.concatenate([high, low], axis=1))
        blend += both[:, :LANES] + both[:, LANES:] + dot(w_halo[1, :, 0:48], high)
        spill = jnp.sum(w_z[...] * spill, axis=1, keepdims=True)
        ahead = pltpu.roll(blend, LANES - 1, 1)
        ahead = jnp.where(iota((rows, LANES), 1) == LANES - 1, spill, ahead)
        mixed = blend + share_y[...] * (ahead - blend)
        sent[now] = mixed.reshape(64, 4, LANES)

        def send(step, carry):
            to = peer(q, step)
            pltpu.make_async_remote_copy(
                src_ref=sent.at[now, to],
                dst_ref=got.at[now, q],
                send_sem=swap_send.at[now],
                recv_sem=swap_recv.at[now],
                device_id={"gx": to},
                device_id_type=MESH,
            ).start()
            return carry

        lax.fori_loop(0, nx - 1, send, 0, unroll=True)
        got[now, pl.ds(q, 1)] = sent[now, pl.ds(q, 1)]

        for first, count, plane in GROUPS:
            a, b, c, d = BACK if count == 32 else BODY
            layers = iota((Z, LANES), 0)

            def step_plane(n, carry, first=first, plane=plane, a=a, b=b, c=c, d=d):
                here = f[first + n]
                side = pltpu.roll(edges, LANES - 2 * (plane + n), 1)
                back_y = pltpu.roll(jnp.where(lane == LANES - 1, side, here), 1, 1)
                ahead_y = pltpu.roll(jnp.where(lane == 0, side, here), LANES - 1, 1)
                back_z = jnp.where(layers == 0, 0.0, pltpu.roll(here, 1, 0))
                ahead_z = jnp.where(layers == Z - 1, 0.0, pltpu.roll(here, Z - 1, 0))
                new = (
                    (1.0 - a - b - c - 6.0 * d) * here
                    + (a + d) * f[first + n - 1]
                    + d * f[first + n + 1]
                    + (b + d) * back_y
                    + d * ahead_y
                    + (c + d) * back_z
                    + d * ahead_z
                )
                if plane == 0:
                    new = new * keep[n // 8, pl.ds(pl.multiple_of(n % 8 * Z, Z), Z)]
                else:
                    new = jnp.where(layers >= Z - 2, 0.0, new)
                moved[plane + n] = new
                return carry

            for n in range(count):
                step_plane(n, 0)

        pltpu.make_async_remote_copy(
            src_ref=sent.at[now, pl.ds(0, nx - 1)],
            dst_ref=got.at[now, pl.ds(0, nx - 1)],
            send_sem=swap_send.at[now],
            recv_sem=swap_recv.at[now],
            device_id={"gx": q_up},
            device_id_type=MESH,
        ).wait_recv()

        high, low = split(got[now].reshape(rows, LANES))
        received = jnp.concatenate([high, low], axis=1)
        for n in (0, 4, 5, 3, 1, 2):
            both = dot(place[n], received)
            added = both[:, :LANES] + both[:, LANES:]
            if n < 4:
                new = moved[8 * n : 8 * n + 8] + added.reshape(8, Z, LANES)
                if final:
                    back_out[8 * n : 8 * n + 8] = new
                else:
                    field[now + 1, 1 + 8 * n : 9 + 8 * n] = new
            else:
                start = 32 + 16 * (n - 4)
                low_part = moved[start : start + 16, 0:8]
                new = moved[start : start + 16, 8:16] + added.reshape(16, 8, LANES)
                if final:
                    body_out[n - 4, :, 0:8] = low_part
                    body_out[n - 4, :, 8:16] = new
                else:
                    first = GROUPS[n - 3][0]
                    field[now + 1, first : first + 16, 0:8] = low_part
                    field[now + 1, first : first + 16, 8:16] = new
            if n == 5 and not final:
                pack_corner(now + 1)
                start_halos(now + 1, (8, 1, 3, 5, 2, 4))
            if n == 3 and not final:
                start_halos(now + 1, (0,))
        if not final:
            pack_edges(now + 1)
            start_halos(now + 1, (6, 7))

    for now in range(STEPS):
        for copy in halo_copies(now):
            copy.wait_send()
        pltpu.make_async_remote_copy(
            src_ref=sent.at[now, pl.ds(0, nx - 1)],
            dst_ref=got.at[now, pl.ds(0, nx - 1)],
            send_sem=swap_send.at[now],
            recv_sem=swap_recv.at[now],
            device_id={"gx": q_up},
            device_id_type=MESH,
        ).wait_send()


def per_device(
    background,
    nearbody,
    donor_rows,
    donor_fractions,
    fringe_slots,
    return_rows,
    return_fractions,
    hole_slots,
):
    nx, ny = lax.axis_size("gx"), lax.axis_size("gy")
    by_slot = lambda rows: jnp.swapaxes(rows[0, 0], 0, 1)
    shares = lambda parts: jnp.swapaxes(parts[:, 0, 0], 1, 2)
    vmem = pl.BlockSpec(memory_space=pltpu.VMEM)
    hbm = pl.BlockSpec(memory_space=pltpu.HBM)
    dma = pltpu.SemaphoreType.DMA
    return pl.pallas_call(
        functools.partial(kernel, nx, ny),
        out_shape=(
            jax.ShapeDtypeStruct(background.shape, F32),
            jax.ShapeDtypeStruct(nearbody.shape, F32),
        ),
        in_specs=[hbm] * 8,
        out_specs=(vmem, vmem),
        scratch_shapes=[
            pltpu.VMEM((2, 64), jnp.int32),
            pltpu.VMEM((3, 2, 64), F32),
            pltpu.VMEM((2, 64), jnp.int32),
            pltpu.VMEM((2, 64), jnp.int32),
            pltpu.VMEM((3, 2, 64), F32),
            pltpu.VMEM((2, 64), jnp.int32),
            pltpu.VMEM((STEPS, PLANES, Z, LANES), F32),
            pltpu.VMEM((64, Z, LANES), F32),
            pltpu.VMEM((24, LANES), F32),
            pltpu.VMEM((4, 256, 2 * LANES), BF16),
            pltpu.VMEM((4, 256, 2 * LANES), BF16),
            pltpu.VMEM((2, 256, LANES), BF16),
            pltpu.VMEM((256, 2 * LANES), BF16),
            pltpu.VMEM((256, LANES), F32),
            pltpu.VMEM((256, LANES), F32),
            pltpu.VMEM((6, LANES, 256), BF16),
            pltpu.VMEM((4, LANES, LANES), F32),
            pltpu.VMEM((STEPS, Z, LANES), F32),
            pltpu.VMEM((STEPS, Z, LANES), F32),
            pltpu.VMEM((STEPS, Z, LANES), F32),
            pltpu.VMEM((STEPS, Z, LANES), F32),
            pltpu.VMEM((STEPS, Z, LANES), F32),
            pltpu.VMEM((STEPS, 64, 4, LANES), F32),
            pltpu.VMEM((STEPS, 64, 4, LANES), F32),
            dma((9,)),
            dma((STEPS, 9)),
            dma((STEPS, 9)),
            dma((STEPS,)),
            dma((STEPS,)),
        ],
        compiler_params=pltpu.CompilerParams(
            collective_id=0, has_side_effects=True, vmem_limit_bytes=32 * 1024 * 1024
        ),
        name="overset_steps",
    )(
        *(
            pltpu.with_memory_space_constraint(operand, pltpu.HBM)
            for operand in (
                background,
                nearbody,
                by_slot(donor_rows),
                shares(donor_fractions),
                by_slot(fringe_slots),
                by_slot(return_rows),
                shares(return_fractions),
                by_slot(hole_slots),
            )
        )
    )


def solution(mesh):
    placed = (
        P("gx", None, "gy"),
        P(None, "gx", None, "gy"),
        P("gx", "gy", None, None),
        P(None, "gx", "gy", None, None),
        P("gx", "gy", None, None),
        P("gx", "gy", None, None),
        P(None, "gx", "gy", None, None),
        P("gx", "gy", None, None),
    )
    return jax.shard_map(
        per_device,
        mesh=mesh,
        in_specs=placed,
        out_specs=(P("gx", None, "gy"), P(None, "gx", None, "gy")),
        check_vma=False,
    )
```

```python
import functools

import jax
import jax.numpy as jnp
from jax import lax
from jax.experimental import pallas as pl
from jax.experimental.pallas import tpu as pltpu
from jax.sharding import PartitionSpec as P

STEPS = 2
MESH = pl.DeviceIdType.MESH

BACK = (0.3, 0.25, 0.15, 0.04)
BODY = (0.2, 0.3, 0.2, 0.045)

GROUPS = ((1, 32, 0), (35, 16, 32), (53, 16, 48))
PLANES = 70
Z = 16
LANES = 128
F32 = jnp.float32
BF16 = jnp.bfloat16


def iota(shape, dim):
    return lax.broadcasted_iota(jnp.int32, shape, dim)


def split(value):
    high = value.astype(BF16)
    return high, (value - high.astype(F32)).astype(BF16)


def dot(a, b):
    return jnp.dot(a, b, preferred_element_type=F32)


def exact_dot(a, b, dims=((1,), (0,))):
    return lax.dot_general(
        a, b, (dims, ((), ())), precision=lax.Precision.HIGHEST, preferred_element_type=F32
    )


def peer(q, step):
    def away(n):
        return 4 + (1 - 2 * (n % 2)) * ((n + 1) // 2)

    return (q // 8 + away(step // 8)) % 8 * 8 + (q % 8 + away(step % 8)) % 8


def kernel(
    nx,
    ny,
    back_ref,
    body_ref,
    donor_rows_ref,
    donor_fractions_ref,
    fringe_slots_ref,
    return_rows_ref,
    return_fractions_ref,
    hole_slots_ref,
    out,
    donor_rows,
    donor_fractions,
    fringe_slots,
    return_rows,
    return_fractions,
    hole_slots,
    field,
    moved,
    table,
    w_high,
    w_low,
    w_halo,
    w_x,
    w_z,
    share_y,
    place,
    keep,
    edge,
    corner,
    edge_above,
    edge_below,
    edge_corner,
    sent,
    got,
    in_sem,
    halo_send,
    halo_recv,
    swap_send,
    swap_recv,
):
    q = lax.axis_index("gx")
    j = lax.axis_index("gy")
    q_up, q_down = lax.rem(q + 1, nx), lax.rem(q + nx - 1, nx)
    j_up, j_down = lax.rem(j + 1, ny), lax.rem(j + ny - 1, ny)

    loads = [
        pltpu.make_async_copy(back_ref, field.at[0, pl.ds(1, 32)], in_sem.at[0]),
        pltpu.make_async_copy(body_ref.at[0], field.at[0, pl.ds(35, 16)], in_sem.at[1]),
        pltpu.make_async_copy(body_ref.at[1], field.at[0, pl.ds(53, 16)], in_sem.at[2]),
    ]
    tables = [
        pltpu.make_async_copy(src, dst, in_sem.at[3 + n])
        for n, (src, dst) in enumerate(
            (
                (donor_rows_ref, donor_rows),
                (donor_fractions_ref, donor_fractions),
                (fringe_slots_ref, fringe_slots),
                (return_rows_ref, return_rows),
                (return_fractions_ref, return_fractions),
                (hole_slots_ref, hole_slots),
            )
        )
    ]
    for load in loads + tables:
        load.start()

    barrier = pltpu.get_barrier_semaphore()

    def greet(step, carry):
        pl.semaphore_signal(barrier, inc=1, device_id={"gx": peer(q, step)}, device_id_type=MESH)
        return carry

    lax.fori_loop(0, nx - 1, greet, 0, unroll=True)
    for there in ((q, j_up), (q, j_down), (q_down, j_down), (q_up, j_up)):
        pl.semaphore_signal(
            barrier, inc=1, device_id={"gx": there[0], "gy": there[1]}, device_id_type=MESH
        )

    def halo_copies(now, which=range(9)):
        f = field.at[now]
        pairs = []
        for n, (first, count, _) in enumerate(GROUPS):
            pairs.append((f.at[first + count - 1], f.at[first - 1], q_up, j))
            pairs.append((f.at[first], f.at[first + count], q_down, j))
        pairs.append((edge.at[now], edge_below.at[now], q, j_up))
        pairs.append((edge.at[now], edge_above.at[now], q, j_down))
        pairs.append((corner.at[now], edge_corner.at[now], q_down, j_down))
        return [
            pltpu.make_async_remote_copy(
                src_ref=src,
                dst_ref=dst,
                send_sem=halo_send.at[now, n],
                recv_sem=halo_recv.at[now, n],
                device_id={"gx": to_q, "gy": to_j},
                device_id_type=MESH,
            )
            for n in which
            for src, dst, to_q, to_j in pairs[n : n + 1]
        ]

    lane = iota((Z, LANES), 1)

    def pack_edges(now):
        packed = jnp.zeros((Z, LANES), F32)
        for first, count, plane in GROUPS:
            for k in range(count):
                spot = 2 * (plane + k)
                rolled = pltpu.roll(field[now, first + k], spot, 1)
                hit = (lane == spot) | (lane == (spot - 1) % LANES)
                packed = jnp.where(hit, rolled, packed)
        edge[now] = packed

    def pack_corner(now):
        packed = jnp.zeros((Z, LANES), F32)
        for n, (first, _, _) in enumerate(GROUPS):
            spot = 2 * n + 1
            packed = jnp.where(lane == spot, pltpu.roll(field[now, first], spot, 1), packed)
        corner[now] = packed

    def start_halos(now, which):
        for copy in halo_copies(now, which):
            copy.start()

    for load in tables:
        load.wait()
    table[...] = jnp.zeros_like(table)
    half = ((donor_rows, return_rows), (fringe_slots, hole_slots))
    for n, (first, second) in enumerate(half):
        table[4 * n : 4 * n + 2, 0:64] = first[...].astype(F32)
        table[4 * n + 2 : 4 * n + 4, 0:64] = second[...].astype(F32)
    for n in range(3):
        table[8 + 4 * n : 10 + 4 * n, 0:64] = donor_fractions[n]
        table[10 + 4 * n : 12 + 4 * n, 0:64] = return_fractions[n]
    rows = 4 * 64
    spread = (iota((LANES, rows), 1) // 4 == iota((LANES, rows), 0)).astype(F32)
    wide = exact_dot(table[...], spread)
    kind = iota((1, rows), 1) % 4

    def pick(n):
        x = wide[4 * n : 4 * n + 4]
        return jnp.where(
            kind == 0, x[0:1], jnp.where(kind == 1, x[1:2], jnp.where(kind == 2, x[2:3], x[3:4]))
        )

    row = jnp.maximum(pick(0), 0.0)
    slot = pick(1)
    donor = kind < 2
    used = jnp.where(donor, float(Z - 1), float(Z - 3))
    plane = jnp.floor((row + 0.5) / used)
    layer = row - plane * used
    plane = jnp.where(donor, plane, plane + 32.0)
    target = jnp.where(slot < 0.0, -1.0, jnp.where(donor, slot + 512.0, slot))
    columns = jnp.concatenate(
        [plane, layer, pick(2), pick(3), pick(4), jnp.zeros((3, rows), F32)], axis=0
    ).T
    plane_c = columns[:, 0:1].astype(jnp.int32)
    layer_c = columns[:, 1:2].astype(jnp.int32)
    f1, f2, f3 = columns[:, 2:3], columns[:, 3:4], columns[:, 4:5]
    share_y[...] = jnp.broadcast_to(f3, (rows, LANES))
    last = (plane_c == 31) | (plane_c == 47) | (plane_c == 63)
    halo_index = jnp.where(plane_c == 31, 0, jnp.where(plane_c == 47, 1, 2))
    w00, w01 = (1.0 - f1) * (1.0 - f2), (1.0 - f1) * f2
    w10, w11 = f1 * (1.0 - f2), f1 * f2
    base = plane_c * Z + layer_c
    far = jnp.where(last, -1000, base + Z)

    def weigh(n, carry):
        k = iota((rows, 2 * LANES), 1) + n * (2 * LANES)
        w = (
            jnp.where(k == base, w00, 0.0)
            + jnp.where(k == base + 1, w01, 0.0)
            + jnp.where(k == far, w10, 0.0)
            + jnp.where(k == far + 1, w11, 0.0)
        )
        high, low = split(w)
        w_high[n] = high
        w_low[n] = low
        return carry

    lax.fori_loop(0, 4, weigh, 0)
    k = iota((rows, LANES), 1)
    near = jnp.where(last, halo_index * Z + layer_c, -1000)
    high, low = split(jnp.where(k == near, w10, 0.0) + jnp.where(k == near + 1, w11, 0.0))
    w_halo[0] = high
    w_halo[1] = low
    beyond = jnp.where(last, 1 + 2 * halo_index, 2 * plane_c + 2)
    high, low = split(
        jnp.where(k == 2 * plane_c, 1.0 - f1, 0.0) + jnp.where(k == beyond, f1, 0.0)
    )
    w_x[...] = jnp.concatenate([high, low], axis=1)
    k = jnp.where(k < 2 * Z, k % Z, -1000)
    w_z[...] = jnp.where(k == layer_c, 1.0 - f2, 0.0) + jnp.where(k == layer_c + 1, f2, 0.0)

    target_i = target.astype(jnp.int32)
    ones = jnp.ones((rows, LANES), BF16)

    def lay_back(n, carry):
        r = iota((LANES, rows), 0) + n * LANES
        hit = jnp.where(r == target_i, 1.0, 0.0).astype(BF16)
        place[n] = hit
        keep[n] = 1.0 - dot(hit, ones)
        return carry

    lax.fori_loop(0, 4, lay_back, 0)

    def lay_body(n, carry):
        r = iota((LANES, rows), 0)
        r = 512 + (r // 8 + n * 16) * Z + 8 + r % 8
        place[4 + n] = jnp.where(r == target_i, 1.0, 0.0).astype(BF16)
        return carry

    lax.fori_loop(0, 2, lay_body, 0)

    for load in loads:
        load.wait()
    pack_corner(0)
    pack_edges(0)
    pl.semaphore_wait(barrier, nx - 1 + 4)
    start_halos(0, (8, 1, 3, 5, 0, 2, 4, 6, 7))

    for now in range(STEPS):
        final = now == STEPS - 1
        f = field.at[now]

        blend = jnp.zeros((rows, LANES), F32)
        for first, count, plane in GROUPS:
            for part in range(count // 16):
                start = first + 16 * part
                high, low = split(f[start : start + 16].reshape(2 * LANES, LANES))
                n = plane // 16 + part
                both = dot(w_high[n], jnp.concatenate([high, low], axis=1))
                blend += both[:, :LANES] + both[:, LANES:] + dot(w_low[n], high)

        for copy in halo_copies(now, range(6)):
            copy.wait_recv()

        zero = jnp.zeros((Z, LANES), F32)
        f[0] = jnp.where(q == 0, zero, f[0])
        f[33] = jnp.where(q == nx - 1, zero, f[33])
        high, low = split(jnp.concatenate([f[33], f[51], f[69]], axis=0))
        both = dot(w_halo[0, :, 0:48], jnp.concatenate([high, low], axis=1))
        blend += both[:, :LANES] + both[:, LANES:] + dot(w_halo[1, :, 0:48], high)
        ahead = pltpu.roll(blend, LANES - 1, 1)

        for copy in halo_copies(now, range(6, 9)):
            copy.wait_recv()
        in_back = lane < 63
        below = jnp.where((j == 0) & (in_back | (lane == 127)), zero, edge_below[now])
        above = jnp.where((j == ny - 1) & in_back, zero, edge_above[now])
        even = lane % 2 == 0
        edges = jnp.where(even, above, below)
        ends = (lane == 1) & ((j == ny - 1) | (q == nx - 1))
        high, low = split(jnp.where(even, above, jnp.where(ends, zero, edge_corner[now])))
        high_y = jnp.concatenate(
            [
                jnp.concatenate([high, high], axis=1),
                jnp.concatenate([low, jnp.zeros((Z, LANES), BF16)], axis=1),
                jnp.zeros((LANES - 2 * Z, 2 * LANES), BF16),
            ],
            axis=0,
        )
        spill = lax.dot_general(
            w_x[...], high_y, (((1,), (1,)), ((), ())), preferred_element_type=F32
        )
        spill = jnp.sum(w_z[...] * spill, axis=1, keepdims=True)
        ahead = jnp.where(iota((rows, LANES), 1) == LANES - 1, spill, ahead)
        mixed = blend + share_y[...] * (ahead - blend)
        sent[now] = mixed.reshape(64, 4, LANES)

        def send(step, carry):
            to = peer(q, step)
            pltpu.make_async_remote_copy(
                src_ref=sent.at[now, to],
                dst_ref=got.at[now, q],
                send_sem=swap_send.at[now],
                recv_sem=swap_recv.at[now],
                device_id={"gx": to},
                device_id_type=MESH,
            ).start()
            return carry

        lax.fori_loop(0, nx - 1, send, 0, unroll=True)
        got[now, pl.ds(q, 1)] = sent[now, pl.ds(q, 1)]

        for first, count, plane in GROUPS:
            a, b, c, d = BACK if count == 32 else BODY
            layers = iota((Z, LANES), 0)

            def step_plane(n, carry, first=first, plane=plane, a=a, b=b, c=c, d=d):
                here = f[first + n]
                side = pltpu.roll(edges, LANES - 2 * (plane + n), 1)
                back_y = pltpu.roll(jnp.where(lane == LANES - 1, side, here), 1, 1)
                ahead_y = pltpu.roll(jnp.where(lane == 0, side, here), LANES - 1, 1)
                back_z = jnp.where(layers == 0, 0.0, pltpu.roll(here, 1, 0))
                ahead_z = jnp.where(layers == Z - 1, 0.0, pltpu.roll(here, Z - 1, 0))
                new = (
                    (1.0 - a - b - c - 6.0 * d) * here
                    + (a + d) * f[first + n - 1]
                    + d * f[first + n + 1]
                    + (b + d) * back_y
                    + d * ahead_y
                    + (c + d) * back_z
                    + d * ahead_z
                )
                if plane == 0:
                    new = new * keep[n // 8, pl.ds(pl.multiple_of(n % 8 * Z, Z), Z)]
                else:
                    new = jnp.where(layers >= Z - 2, 0.0, new)
                moved[plane + n] = new
                return carry

            for n in range(count):
                step_plane(n, 0)

        pltpu.make_async_remote_copy(
            src_ref=sent.at[now, pl.ds(0, nx - 1)],
            dst_ref=got.at[now, pl.ds(0, nx - 1)],
            send_sem=swap_send.at[now],
            recv_sem=swap_recv.at[now],
            device_id={"gx": q_up},
            device_id_type=MESH,
        ).wait_recv()

        high, low = split(got[now].reshape(rows, LANES))
        received = jnp.concatenate([high, low], axis=1)
        for n in (0, 4, 5, 3, 1, 2):
            both = dot(place[n], received)
            added = both[:, :LANES] + both[:, LANES:]
            if n < 4:
                new = moved[8 * n : 8 * n + 8] + added.reshape(8, Z, LANES)
                if final:
                    out[8 * n : 8 * n + 8] = new
                else:
                    field[now + 1, 1 + 8 * n : 9 + 8 * n] = new
            else:
                start = 32 + 16 * (n - 4)
                low_part = moved[start : start + 16, 0:8]
                new = moved[start : start + 16, 8:16] + added.reshape(16, 8, LANES)
                if final:
                    out[start : start + 16, 0:8] = low_part
                    out[start : start + 16, 8:16] = new
                else:
                    first = GROUPS[n - 3][0]
                    field[now + 1, first : first + 16, 0:8] = low_part
                    field[now + 1, first : first + 16, 8:16] = new
            if n == 5 and not final:
                pack_corner(now + 1)
                start_halos(now + 1, (8, 1, 3, 5, 2, 4))
            if n == 3 and not final:
                start_halos(now + 1, (0,))
        if not final:
            pack_edges(now + 1)
            start_halos(now + 1, (6, 7))

    for now in range(STEPS):
        for copy in halo_copies(now):
            copy.wait_send()
        pltpu.make_async_remote_copy(
            src_ref=sent.at[now, pl.ds(0, nx - 1)],
            dst_ref=got.at[now, pl.ds(0, nx - 1)],
            send_sem=swap_send.at[now],
            recv_sem=swap_recv.at[now],
            device_id={"gx": q_up},
            device_id_type=MESH,
        ).wait_send()


def per_device(
    background,
    nearbody,
    donor_rows,
    donor_fractions,
    fringe_slots,
    return_rows,
    return_fractions,
    hole_slots,
):
    nx, ny = lax.axis_size("gx"), lax.axis_size("gy")
    by_slot = lambda rows: jnp.swapaxes(rows[0, 0], 0, 1)
    shares = lambda parts: jnp.swapaxes(parts[:, 0, 0], 1, 2)
    vmem = pl.BlockSpec(memory_space=pltpu.VMEM)
    hbm = pl.BlockSpec(memory_space=pltpu.HBM)
    dma = pltpu.SemaphoreType.DMA
    fields = pl.pallas_call(
        functools.partial(kernel, nx, ny),
        out_shape=jax.ShapeDtypeStruct((64, Z, LANES), F32),
        in_specs=[hbm] * 8,
        out_specs=vmem,
        scratch_shapes=[
            pltpu.VMEM((2, 64), jnp.int32),
            pltpu.VMEM((3, 2, 64), F32),
            pltpu.VMEM((2, 64), jnp.int32),
            pltpu.VMEM((2, 64), jnp.int32),
            pltpu.VMEM((3, 2, 64), F32),
            pltpu.VMEM((2, 64), jnp.int32),
            pltpu.VMEM((STEPS, PLANES, Z, LANES), F32),
            pltpu.VMEM((64, Z, LANES), F32),
            pltpu.VMEM((24, LANES), F32),
            pltpu.VMEM((4, 256, 2 * LANES), BF16),
            pltpu.VMEM((4, 256, 2 * LANES), BF16),
            pltpu.VMEM((2, 256, LANES), BF16),
            pltpu.VMEM((256, 2 * LANES), BF16),
            pltpu.VMEM((256, LANES), F32),
            pltpu.VMEM((256, LANES), F32),
            pltpu.VMEM((6, LANES, 256), BF16),
            pltpu.VMEM((4, LANES, LANES), F32),
            pltpu.VMEM((STEPS, Z, LANES), F32),
            pltpu.VMEM((STEPS, Z, LANES), F32),
            pltpu.VMEM((STEPS, Z, LANES), F32),
            pltpu.VMEM((STEPS, Z, LANES), F32),
            pltpu.VMEM((STEPS, Z, LANES), F32),
            pltpu.VMEM((STEPS, 64, 4, LANES), F32),
            pltpu.VMEM((STEPS, 64, 4, LANES), F32),
            dma((9,)),
            dma((STEPS, 9)),
            dma((STEPS, 9)),
            dma((STEPS,)),
            dma((STEPS,)),
        ],
        compiler_params=pltpu.CompilerParams(
            collective_id=0, has_side_effects=True, vmem_limit_bytes=32 * 1024 * 1024
        ),
        name="overset_steps",
    )(
        *(
            pltpu.with_memory_space_constraint(operand, pltpu.HBM)
            for operand in (
                background,
                nearbody,
                by_slot(donor_rows),
                shares(donor_fractions),
                by_slot(fringe_slots),
                by_slot(return_rows),
                shares(return_fractions),
                by_slot(hole_slots),
            )
        )
    )
    return fields[:32], fields[32:].reshape(nearbody.shape)


def solution(mesh):
    placed = (
        P("gx", None, "gy"),
        P(None, "gx", None, "gy"),
        P("gx", "gy", None, None),
        P(None, "gx", "gy", None, None),
        P("gx", "gy", None, None),
        P("gx", "gy", None, None),
        P(None, "gx", "gy", None, None),
        P("gx", "gy", None, None),
    )
    return jax.shard_map(
        per_device,
        mesh=mesh,
        in_specs=placed,
        out_specs=(P("gx", None, "gy"), P(None, "gx", None, "gy")),
        check_vma=False,
    )
```
